32 devices in a mesh: groups: 2 (over y), seq: 4 (over z), phase: 4 (over x, core).
Axes of the slice: x: 2, y: 2, z: 4, core: 2. Of those that a mesh axis runs over, the one named last changes fastest.
Arguments:
- phase_rows: bfloat16 [4, 512, 3072], P('phase', ('groups', 'seq')), parts along dimension 1, may hold values from -6 to 6
- fresh_rows: bfloat16 [512, 3072], P(('groups', 'seq')), parts along dimension 0, may hold values from -6 to 6
- token_counts: int32 [10], P('groups'), parts along dimension 0, may hold values from 2 to 256, as said below
- memory: float32 [4, 384, 3072], P('phase', 'groups', 'seq'), parts along dimension 1, may hold values from -24 to 24
- normalizer: float32 [4, 384], P('phase', 'groups'), parts along dimension 1, may hold values from 0.05 to 0.5
- w_memq: bfloat16 [4, 3072, 32], P('phase'), may hold values from -0.109375 to 0.109375
- w_memk: bfloat16 [4, 3072, 32], P('phase'), may hold values from -0.109375 to 0.109375
- norm_gain: float32 [4, 3072], P('phase'), may hold values from 0.5 to 1.5
- w_kv: bfloat16 [4, 3072, 1024], P('phase', 'seq'), may hold values from -2 to 2
- w_out: bfloat16 [4, 512, 3072], P('phase', 'seq'), may hold values from -0.25 to 0.25
Outputs:
- rows_out: bfloat16 [4, 512, 3072], P('phase', ('groups', 'seq')), parts along dimension 1
- memory_out: float32 [4, 384, 3072], P('phase', 'groups', 'seq'), parts along dimension 1
- normalizer_out: float32 [4, 384], P('phase', 'groups'), parts along dimension 1
The draws below stay inside these ranges and needn't reach their ends.
There are 2 independent parts, one for each index of `groups`. The reference program is written for one: setup_inputs(seed, part) draws one part's arguments, and reference() takes and returns one part's arrays. A program takes and returns all parts, laid end to end along the dimension named above; an argument that names none is the same for every part. Nothing has to cross between parts.
Inputs may be any that keep to these rules, and one draw needn't show every extreme that they name: token_counts[0] counts the valid tokens of the segment entering section 0 in the second step and token_counts[s + 1] those of the segment at section s in the first step; valid tokens are the first ones of a segment; at least one entry equals 256.
All inputs are finite; a program needn't handle non-finite values.
Results may differ from the reference program's by a relative error of at most 0.024.
Values may be sent and summed in bfloat16 or wider, within the bound.
A program may use at most 64 MiB of HBM per device.

```python
import math
import jax
import jax.numpy as jnp
from jax import lax

D = 3072
HEAD_DIM = 128
KV_HEADS = 4
KEY_DIM = 32
TOK_DEV = 64
KVW = 512
MEM = 192
SEG = 256
N_SEQ = 4
N_PHASE = 4


def draw_token_counts(key, part):
    key = jax.random.fold_in(key, 7)
    first_key, second_key, third_key = jax.random.split(key, 3)
    partial_counts = jax.random.randint(first_key, (N_PHASE + 1,), 2, SEG + 1)
    full_flags = jax.random.randint(second_key, (N_PHASE + 1,), 0, 2)
    counts = jnp.where(full_flags == 1, SEG, partial_counts)
    chosen = jax.random.randint(third_key, (), 0, N_PHASE + 1)
    return jnp.where(jnp.arange(N_PHASE + 1) == chosen, SEG, counts).astype(jnp.int32)


def draw_phase_rows(key, part):
    key = jax.random.fold_in(key, 11)
    base_key = jax.random.fold_in(key, 0)
    row_shape = (N_PHASE, SEG, D)
    base_rows = jnp.clip(jax.random.normal(base_key, row_shape, jnp.float32), -6.0, 6.0)
    return base_rows.astype(jnp.bfloat16)


def draw_fresh_rows(key, part):
    key = jax.random.fold_in(key, 12)
    base_key = jax.random.fold_in(key, 0)
    row_shape = (SEG, D)
    base_rows = jnp.clip(jax.random.normal(base_key, row_shape, jnp.float32), -6.0, 6.0)
    return base_rows.astype(jnp.bfloat16)


def draw_w_kv(key, part):
    key = jax.random.fold_in(key, 13)
    base_key = jax.random.fold_in(key, 0)
    weight_shape = (N_PHASE, D, 2 * KVW)
    spread = 1.0 / math.sqrt(D)
    entries = jnp.clip(jax.random.normal(base_key, weight_shape, jnp.float32), -6.0, 6.0) * spread
    return entries.astype(jnp.bfloat16)


def steps_of(key, extent, cuts, least, top_value):
    def one(axis_at, blocks):
        heights = jax.random.uniform(jax.random.fold_in(jax.random.fold_in(key, 6), axis_at), (blocks,), jnp.float32, least / len(cuts), top_value / len(cuts))
        return jnp.repeat(jnp.exp(heights), extent[axis_at] // blocks).reshape((-1,) + (1,) * (len(extent) - axis_at - 1))

    gain = one(*cuts[0])
    for cut in cuts[1:]:
        gain = gain * one(*cut)
    return gain


def gaussian(rng, extent, width, most, cuts=(), held_as=jnp.bfloat16):
    result = width * jax.random.normal(rng, extent, jnp.float32)
    if cuts:
        result = result * steps_of(rng, extent, cuts, -0.22, 0.18)
    return jnp.clip(result, -most, most).astype(held_as)


def setup_inputs(seed: int = 0, part: int = 0) -> dict:
    key_list = jax.random.split(jax.random.key(seed), 11)
    own_keys = jax.random.split(jax.random.fold_in(key_list[10], part), 11)
    return {
        "phase_rows": draw_phase_rows(jax.random.fold_in(jax.random.fold_in(key_list[10], part), 71), part),
        "fresh_rows": draw_fresh_rows(jax.random.fold_in(jax.random.fold_in(key_list[10], part), 71), part),
        "token_counts": draw_token_counts(jax.random.fold_in(jax.random.fold_in(key_list[10], part), 71), part),
        "memory": gaussian(own_keys[3], (N_PHASE, MEM, D), 4.0, 24.0, ((0, 4), (2, 4)), jnp.float32),
        "normalizer": jnp.clip(jnp.exp(math.log(0.5) - 2.3025851 * jax.random.uniform(own_keys[4], (N_PHASE, MEM), jnp.float32) ** steps_of(own_keys[4], (N_PHASE, MEM), ((0, 4),), -0.2, 0.2)), 0.05, 0.5),
        "w_memq": gaussian(key_list[5], (N_PHASE, D, KEY_DIM), D ** -0.5, 0.109375, ((0, 4),)),
        "w_memk": gaussian(key_list[6], (N_PHASE, D, KEY_DIM), D ** -0.5, 0.109375, ((0, 4),)),
        "norm_gain": jnp.clip(1.0 + 0.1 * jax.random.normal(key_list[7], (N_PHASE, D), jnp.float32), 0.5, 1.5),
        "w_kv": draw_w_kv(jax.random.fold_in(key_list[10], 71), part),
        "w_out": gaussian(key_list[9], (N_PHASE, KVW, D), KVW ** -0.5, 0.25, ((0, 4), (1, 4))),
    }


PRECISE = lax.Precision.HIGHEST

def features(projected):
    halves = jnp.concatenate([jax.nn.relu(projected), jax.nn.relu(-projected)], axis=-1)
    return jnp.concatenate([halves * jnp.roll(halves, offset, axis=-1) for offset in (1, 2, 3)], axis=-1)

def recall(feature_rows, memory_state, norm_state):
    numerator = jnp.dot(feature_rows, memory_state, precision=PRECISE)
    denominator = jnp.dot(feature_rows, norm_state, precision=PRECISE) + 1.0
    return numerator / denominator[:, None]

def block_sum(terms):
    rounded = terms.astype(jnp.bfloat16)
    rounded = lax.optimization_barrier(rounded)
    return lax.optimization_barrier(jnp.sum(rounded.astype(jnp.float32), axis=0))

def section(in_rows, valid_count, memory_state, norm_state, w_memq, w_memk, norm_gain, w_kv, w_out):
    query_features = features(jnp.dot(in_rows, w_memq, preferred_element_type=jnp.float32))
    residual = in_rows.astype(jnp.float32) + recall(query_features, memory_state, norm_state)
    inverse_rms = lax.rsqrt(lax.optimization_barrier(jnp.mean(residual * residual, axis=-1, keepdims=True)) + 1e-05)
    normed = (residual * inverse_rms * norm_gain).astype(jnp.bfloat16)
    keyval = jnp.dot(normed, w_kv, preferred_element_type=jnp.float32).astype(jnp.bfloat16)
    key_rows = keyval[:, :KVW].astype(jnp.float32).reshape(SEG, KV_HEADS, HEAD_DIM)
    value_rows = keyval[:, KVW:].astype(jnp.float32).reshape(SEG, KV_HEADS, HEAD_DIM)
    position = jnp.arange(SEG)
    allowed = (position[None, :] < valid_count) & (position[None, :] != position[:, None])

    def head_attention(pair):
        head_keys, head_values = pair
        scores = jnp.dot(head_keys, head_keys.T, precision=PRECISE) / math.sqrt(HEAD_DIM)
        scores = jnp.where(allowed, scores, -jnp.inf)
        weights = jax.nn.softmax(scores, axis=-1)
        return jnp.dot(weights, head_values, precision=PRECISE)
    attended = lax.map(head_attention, (jnp.transpose(key_rows, (1, 0, 2)), jnp.transpose(value_rows, (1, 0, 2))))
    attended = jnp.transpose(attended, (1, 0, 2)).reshape(SEG, KVW).astype(jnp.bfloat16)
    output = (residual + jnp.dot(attended, w_out, preferred_element_type=jnp.float32)).astype(jnp.bfloat16)
    key_features = features(jnp.dot(output, w_memk, preferred_element_type=jnp.float32))
    live_rows = (position < valid_count).astype(jnp.float32)[:, None]
    correction = (output.astype(jnp.float32) - recall(key_features, memory_state, norm_state)) * live_rows
    key_features = key_features * live_rows
    feature_blocks = key_features.reshape(N_SEQ, TOK_DEV, MEM)
    correction_blocks = correction.reshape(N_SEQ, TOK_DEV, D)
    update = block_sum(jnp.einsum('btm,btd->bmd', feature_blocks, correction_blocks, precision=PRECISE))
    counted = block_sum(lax.optimization_barrier(jnp.sum(feature_blocks, axis=1)))
    return (output, update, counted)

def reference(phase_rows, fresh_rows, token_counts, memory, normalizer, w_memq, w_memk, norm_gain, w_kv, w_out):
    first_pass = []
    for number in range(N_PHASE):
        first_pass.append(section(phase_rows[number], token_counts[number + 1], memory[number], normalizer[number], w_memq[number], w_memk[number], norm_gain[number], w_kv[number], w_out[number]))
    later_memory = memory + jnp.stack([entry[1] for entry in first_pass])
    later_normalizer = normalizer + jnp.stack([entry[2] for entry in first_pass])
    inputs = [fresh_rows] + [first_pass[number][0] for number in range(N_PHASE - 1)]
    second = []
    for number in range(N_PHASE):
        second.append(section(inputs[number], token_counts[number], later_memory[number], later_normalizer[number], w_memq[number], w_memk[number], norm_gain[number], w_kv[number], w_out[number]))
    rows_out = jnp.stack([entry[0] for entry in second])
    memory_out = later_memory + jnp.stack([entry[1] for entry in second])
    normalizer_out = later_normalizer + jnp.stack([entry[2] for entry in second])
    return (rows_out, memory_out, normalizer_out)
```

```python
import functools
import math

import jax
import jax.numpy as jnp
import numpy as np
from jax import lax
from jax.experimental import pallas as pl
from jax.experimental.pallas import tpu as pltpu
from jax.sharding import PartitionSpec as P

HEAD_DIM = 128


PRECISE = lax.Precision.HIGHEST


def from_behind(value, axis, steps):
    count = lax.axis_size(axis)
    first, last = (max(0, -steps), min(count, count - steps))
    return lax.ppermute(value, axis, [(source, source + steps) for source in range(first, last)])


def features(projected):
    halves = jnp.concatenate([jax.nn.relu(projected), jax.nn.relu(-projected)], axis=-1)
    return jnp.concatenate(
        [halves * jnp.roll(halves, offset, axis=-1) for offset in (1, 2, 3)], axis=-1
    )


def recall(feature_rows, memory_state, norm_state):
    numerator = jnp.dot(feature_rows, memory_state, precision=PRECISE)
    denominator = jnp.dot(feature_rows, norm_state, precision=PRECISE) + 1.0
    return numerator / denominator[:, None]


def attend(keyval, valid_count, position, head_count):
    token_rows = keyval.shape[0]
    kv_width = head_count * HEAD_DIM
    queries = keyval[:, :kv_width].reshape(token_rows, head_count, HEAD_DIM)
    divisor = math.sqrt(HEAD_DIM)

    def absorb_block(running, block_rows, first_row):
        highest, summed, weighted = running
        piece_rows = block_rows.shape[0]
        piece_keys = block_rows[:, :kv_width].reshape(piece_rows, head_count, HEAD_DIM)
        piece_values = (
            block_rows[:, kv_width:].reshape(piece_rows, head_count, HEAD_DIM).astype(jnp.float32)
        )
        scores = (
            jnp.einsum("qhd,khd->hqk", queries, piece_keys, preferred_element_type=jnp.float32)
            / divisor
        )
        key_position = first_row + jnp.arange(piece_rows)
        allowed = (key_position[None, :] < valid_count) & (
            key_position[None, :] != position[:, None]
        )
        masked = jnp.where(allowed[None], scores, -1e30)
        new_highest = jnp.maximum(highest, jnp.max(masked, axis=-1))
        weights = jnp.where(allowed[None], jnp.exp(masked - new_highest[..., None]), 0.0)
        shrink = jnp.exp(highest - new_highest)
        summed = summed * shrink + jnp.sum(weights, axis=-1)
        weighted = weighted * shrink[..., None] + jnp.einsum(
            "hqk,khd->hqd", weights, piece_values, precision=PRECISE
        )
        return (new_highest, summed, weighted)

    initial = (
        jnp.full((head_count, token_rows), -1e30, jnp.float32),
        jnp.zeros((head_count, token_rows), jnp.float32),
        jnp.zeros((head_count, token_rows, HEAD_DIM), jnp.float32),
    )
    running = initial
    shard_rows = lax.all_gather(keyval, "seq", axis=0, tiled=True)
    piece_rows = shard_rows.shape[0]
    block = piece_rows
    while block > 1024 and block % 2 == 0:
        block = block // 2
    block_count = piece_rows // block
    blocks = shard_rows.reshape(block_count, block, shard_rows.shape[1])
    starts = block * jnp.arange(block_count, dtype=jnp.int32)

    def one_block(carry, item):
        block_rows, block_start = item
        return (absorb_block(carry, block_rows, block_start), None)

    running, unused = lax.scan(one_block, running, (blocks, starts))
    highest, summed, weighted = running
    attended = weighted / summed[..., None]
    return jnp.transpose(attended, (1, 0, 2)).reshape(token_rows, kv_width).astype(jnp.bfloat16)


def run_section(in_rows, valid_count, reader, position, params):
    w_memq, w_memk, norm_gain, weights_full, out_full = params
    head_count = out_full.shape[0] // HEAD_DIM
    query_features = features(jnp.dot(in_rows, w_memq, preferred_element_type=jnp.float32))
    residual = in_rows.astype(jnp.float32) + reader(query_features)
    inverse_rms = lax.rsqrt(jnp.mean(residual * residual, axis=-1, keepdims=True) + 1e-05)
    normed = (residual * inverse_rms * norm_gain).astype(jnp.bfloat16)
    keyval = jnp.dot(normed, weights_full, preferred_element_type=jnp.float32).astype(jnp.bfloat16)
    attended = attend(keyval, valid_count, position, head_count)
    output = (residual + jnp.dot(attended, out_full, preferred_element_type=jnp.float32)).astype(
        jnp.bfloat16
    )
    key_features = features(jnp.dot(output, w_memk, preferred_element_type=jnp.float32))
    live_rows = (position < valid_count).astype(jnp.float32)[:, None]
    correction = (output.astype(jnp.float32) - reader(key_features)) * live_rows
    key_features = key_features * live_rows
    update = lax.dot_general(key_features, correction, (((0,), (0,)), ((), ())), precision=PRECISE)
    return (output, update, jnp.sum(key_features, axis=0))


def per_device(
    phase_rows, fresh_rows, token_counts, memory, normalizer, w_memq, w_memk, norm_gain, w_kv, w_out
):
    token_rows = phase_rows.shape[1]
    section_index = lax.axis_index("phase")
    seq_index = lax.axis_index("seq")
    position = seq_index * token_rows + jnp.arange(token_rows)
    weights_full, out_full = (
        lax.all_gather(w_kv[0], "seq", axis=0, tiled=True),
        lax.all_gather(w_out[0], "seq", axis=0, tiled=True),
    )
    memory_cols = memory[0]
    column_width = memory_cols.shape[1]
    memory_full = lax.all_gather(memory_cols, "seq", axis=1, tiled=True)
    norm_now = normalizer[0]
    params = (w_memq[0], w_memk[0], norm_gain[0], weights_full, out_full)

    def first_reader(feature_rows):
        return recall(feature_rows, memory_full, norm_now)

    first_rows, first_update, first_counts = run_section(
        phase_rows[0], token_counts[section_index + 1], first_reader, position, params
    )
    summed, counted = (
        lax.psum(first_update.astype(jnp.bfloat16), "seq").astype(jnp.float32),
        lax.psum(first_counts.astype(jnp.bfloat16), "seq").astype(jnp.float32),
    )
    later_full = memory_full + summed
    later_norm = norm_now + counted
    later_cols = lax.dynamic_slice_in_dim(later_full, seq_index * column_width, column_width, 1)

    def later_reader(feature_rows):
        return recall(feature_rows, later_full, later_norm)

    incoming = from_behind(first_rows, "phase", 1)
    second_in = jnp.where(section_index == 0, fresh_rows, incoming)
    second_rows, second_update, second_counts = run_section(
        second_in, token_counts[section_index], later_reader, position, params
    )
    final_share = lax.psum_scatter(
        second_update.astype(jnp.bfloat16), "seq", scatter_dimension=1, tiled=True
    ).astype(jnp.float32)
    final_counts = lax.psum(second_counts.astype(jnp.bfloat16), "seq").astype(jnp.float32)
    return (second_rows[None], (later_cols + final_share)[None], (later_norm + final_counts)[None])


MESH = pl.DeviceIdType.MESH
NN = (((1,), (0,)), ((), ()))
NT = (((1,), (1,)), ((), ()))
TN = (((0,), (0,)), ((), ()))
(X_IN, P_IN, WOUT, FRESH, P_FRESH, KV, SQ, ATT, PK) = range(9)
ROWS = 13
N_KINDS = 14


def mxu(left, right, dims, precision=None):
    return lax.dot_general(
        left, right, dims, precision=precision, preferred_element_type=jnp.float32
    )


def selection(key_dim):
    width = 2 * key_dim
    select = np.zeros((6 * width, key_dim), np.float32)
    for number in range(3 * width):
        offset, place = number // width + 1, number % width
        for half, entry in ((0, place), (1, (place - offset) % width)):
            select[half * 3 * width + number, entry % key_dim] = 1.0 if entry < key_dim else -1.0
    return select


def columns_kernel(
    n,
    n_phase,
    rows_hbm,
    fresh_hbm,
    counts_ref,
    memory_hbm,
    norm_ref,
    memq_hbm,
    memk_hbm,
    gain_ref,
    wkv_hbm,
    wout_hbm,
    select_ref,
    rows_out,
    memory_out,
    norm_out,
    x1,
    x2,
    own_rows,
    own_fresh,
    memq,
    memk,
    wkv,
    wout,
    mem1,
    mem2,
    key_w,
    query_w,
    next_w,
    p_in,
    p_fresh,
    p_second,
    pq_out,
    resid,
    kv_out,
    kv_in,
    squares,
    att,
    pk,
    out1,
    out2,
    send,
    recv,
    phase_send,
    phase_recv,
    local,
):
    me, ph = lax.axis_index("seq"), lax.axis_index("phase")
    rows, cols = own_rows.shape[0], x1.shape[1]
    width, depth = own_rows.shape[1], memq.shape[1]
    kvw = wkv.shape[1] // 2
    seg = n * rows
    peers = [lax.rem(me + d, n) for d in range(n)]
    origins = [lax.rem(me - d + n, n) for d in range(n)]
    has_next, has_prev = ph < n_phase - 1, ph > 0

    def columns(index):
        return pl.ds(pl.multiple_of(index * cols, cols), cols)

    def block(index):
        return pl.ds(pl.multiple_of(index * rows, rows), rows)

    def head(index, first=0):
        return pl.ds(pl.multiple_of(first + index * HEAD_DIM, HEAD_DIM), HEAD_DIM)

    def to_peer(kind, d, src, dst):
        return pltpu.make_async_remote_copy(
            src_ref=src,
            dst_ref=dst,
            send_sem=send.at[kind, d],
            recv_sem=recv.at[kind, d],
            device_id={"seq": peers[d]},
            device_id_type=MESH,
        )

    def to_phase(kind, step, src, dst):
        return pltpu.make_async_remote_copy(
            src_ref=src,
            dst_ref=dst,
            send_sem=phase_send.at[kind],
            recv_sem=phase_recv.at[kind],
            device_id={"phase": ph + step},
            device_id_type=MESH,
        )

    def here(number, src, dst):
        return pltpu.make_async_copy(src, dst, local.at[number])

    loads = [
        here(0, rows_hbm.at[0], own_rows),
        here(1, memq_hbm.at[0], memq),
        here(2, memory_hbm.at[0], mem1),
        here(3, rows_hbm.at[0, :, columns(me)], x1.at[block(me)]),
        here(4, wkv_hbm.at[0], wkv),
        here(5, memk_hbm.at[0], memk),
        here(6, wout_hbm.at[0, :, columns(me)], wout.at[me]),
        here(7, fresh_hbm, own_fresh),
        here(8, fresh_hbm.at[:, columns(me)], x2.at[block(me)]),
    ]
    for copy in loads[:8]:
        copy.start()

    barrier = pltpu.get_barrier_semaphore()
    for d in range(1, n):
        pl.semaphore_signal(barrier, inc=1, device_id={"seq": peers[d]}, device_id_type=MESH)

    @pl.when(has_next)
    def _():
        pl.semaphore_signal(barrier, inc=1, device_id={"phase": ph + 1}, device_id_type=MESH)

    @pl.when(has_prev)
    def _():
        pl.semaphore_signal(barrier, inc=1, device_id={"phase": ph - 1}, device_id_type=MESH)

    pl.semaphore_wait(barrier, n - 1 + has_next.astype(jnp.int32) + has_prev.astype(jnp.int32))

    sent = []
    x_copies = [
        to_peer(X_IN, d, rows_hbm.at[0, :, columns(peers[d])], x1.at[block(me)])
        for d in range(1, n)
    ]
    fresh_copies = [
        to_peer(FRESH, d, fresh_hbm.at[:, columns(peers[d])], x2.at[block(me)])
        for d in range(1, n)
    ]
    wout_copies = [
        to_peer(WOUT, d, wout_hbm.at[0, :, columns(peers[d])], wout.at[me]) for d in range(1, n)
    ]
    p_copies = [to_peer(P_IN, d, p_in.at[me], p_in.at[me]) for d in range(1, n)]
    pf_copies = [to_peer(P_FRESH, d, p_fresh.at[me], p_fresh.at[me]) for d in range(1, n)]
    for copy in x_copies:
        copy.start()
    sent += x_copies + wout_copies + p_copies

    line = lax.broadcasted_iota(jnp.int32, (depth, depth), 0)
    unit = (line == lax.broadcasted_iota(jnp.int32, (depth, depth), 1)).astype(jnp.bfloat16)
    loads[1].wait()
    query_w[...] = mxu(unit, memq[...], NT).astype(jnp.bfloat16)
    loads[0].wait()
    p_in[me] = mxu(query_w[...], own_rows[...], NT)
    for copy in p_copies:
        copy.start()
    weight_copy = to_phase(0, -1, query_w.at[:, columns(me)], next_w)

    @pl.when(has_prev)
    def _():
        weight_copy.start()

    loads[7].wait()

    @pl.when(ph == 0)
    def _():
        loads[8].start()
        p_fresh[me] = mxu(query_w[...], own_fresh[...], NT)
        for copy in pf_copies + fresh_copies:
            copy.start()

    for copy in wout_copies:
        copy.start()

    loads[5].wait()
    key_w[...] = mxu(unit, memk[...], NT).astype(jnp.bfloat16)

    def across(projected):
        pairs = mxu(select_ref[...], projected, NN, PRECISE)
        pairs = jnp.maximum(pairs, 0.0)
        half = pairs.shape[0] // 2
        return pairs[:half] * pairs[half:]

    def recalled(turned, mem_ref, norm_row):
        upright = turned.T
        scale = jnp.sum(upright * norm_row, axis=1, keepdims=True) + 1.0
        found = mxu(upright.astype(jnp.bfloat16), mem_ref[...].astype(jnp.bfloat16), NN)
        return found / scale, upright

    def section(step, x_ref, projected, mem_ref, norm_row, valid, out_ref, after_output):
        base = 4 * step
        found, _ = recalled(across(projected), mem_ref, norm_row)
        residual = x_ref[...].astype(jnp.float32) + found
        resid[...] = residual
        square = jnp.sum(residual * residual, axis=1, keepdims=True)
        squares[step, me] = jnp.broadcast_to(square, (seg, 128)).T[:8]
        copies = []
        for d in range(1, n):
            copy = to_peer(SQ + base, d, squares.at[step, me], squares.at[step, me])
            copy.start()
            copies.append(copy)
        scaled = (residual * gain_ref[:, columns(me)]).astype(jnp.bfloat16)
        if step == 0:
            loads[4].wait()

        def part(index):
            keys = mxu(scaled, wkv[:, head(index)], NN)
            values = mxu(scaled, wkv[:, head(index, kvw)], NN)
            return jnp.concatenate([keys, values], axis=1)

        for d in range(1, n):
            kv_out[step, d] = part(peers[d]).astype(jnp.bfloat16)
            copy = to_peer(KV + base, d, kv_out.at[step, d], kv_in.at[step, me])
            copy.start()
            copies.append(copy)
        total = part(me)
        sums = squares[step, me]
        for copy in copies:
            copy.wait_recv()
        for d in range(1, n):
            total = total + kv_in[step, origins[d]].astype(jnp.float32)
            sums = sums + squares[step, origins[d]]
        inverse = lax.rsqrt(sums[:1] / width + 1e-05)
        inverse = jnp.broadcast_to(inverse, (128, seg)).T
        keys = (total[:, :HEAD_DIM] * inverse).astype(jnp.bfloat16)
        values = (total[:, HEAD_DIM:] * inverse).astype(jnp.bfloat16)
        scores = mxu(keys, keys, NT) / math.sqrt(HEAD_DIM)
        row_at = lax.broadcasted_iota(jnp.int32, (seg, seg), 0)
        key_at = lax.broadcasted_iota(jnp.int32, (seg, seg), 1)
        scores = jnp.where((key_at < valid) & (key_at != row_at), scores, -1e30)
        weights = jnp.exp(scores - jnp.max(scores, axis=1, keepdims=True))
        weight_sum = jnp.sum(weights, axis=1, keepdims=True)
        attended = mxu(weights.astype(jnp.bfloat16), values, NN) / weight_sum
        att[step, me] = attended.astype(jnp.bfloat16)
        att_copies = []
        for d in range(1, n):
            copy = to_peer(ATT + base, d, att.at[step, me], att.at[step, me])
            copy.start()
            att_copies.append(copy)
        if step == 0:
            loads[6].wait()
            for copy in wout_copies:
                copy.wait_recv()
        resid[...] += mxu(att[step, me], wout[me], NN)
        for d in range(1, n):
            att_copies[d - 1].wait_recv()
            resid[...] += mxu(att[step, origins[d]], wout[origins[d]], NN)
        output = resid[...].astype(jnp.bfloat16)
        out_ref[...] = output
        if step == 0:

            @pl.when(has_next)
            def _():
                weight_in.wait_recv()

            pk[step, me, pl.ds(depth, depth)] = mxu(next_w[...], output, NT)
        pk[step, me, pl.ds(0, depth)] = mxu(key_w[:, columns(me)], output, NT)
        taken = pl.ds(0, (2 - step) * depth)
        pk_copies = []
        for d in range(1, n):
            copy = to_peer(PK + base, d, pk.at[step, me, taken], pk.at[step, me, taken])
            copy.start()
            pk_copies.append(copy)
        after_output()
        for copy in pk_copies:
            copy.wait_recv()
        projected = pk[step, 0, taken]
        for index in range(1, n):
            projected = projected + pk[step, index, taken]
        if step == 0:
            pq_out[...] = projected[depth:]

            @pl.when(has_next)
            def _():
                pq_copy.start()

        turned = across(projected[:depth])
        found, upright = recalled(turned, mem_ref, norm_row)
        live = (lax.broadcasted_iota(jnp.int32, (seg, 1), 0) < valid).astype(jnp.float32)
        correction = (out_ref[...].astype(jnp.float32) - found) * live
        update = mxu(turned.astype(jnp.bfloat16), correction.astype(jnp.bfloat16), NN)
        counted = jnp.sum(upright * live, axis=0, keepdims=True)
        sent.extend(copies + att_copies + pk_copies)
        return update, counted

    weight_in = to_phase(0, -1, query_w.at[:, columns(me)], next_w)
    out_copy = to_phase(1, 1, out1, x2)
    pq_copy = to_phase(2, 1, pq_out, p_second)

    @pl.when(ph == n_phase - 1)
    def _():
        next_w[...] = jnp.zeros_like(next_w)

    loads[2].wait()
    loads[3].wait()
    for copy in p_copies + x_copies:
        copy.wait_recv()

    def joined(ref):
        return jnp.concatenate([ref[index] for index in range(n)], axis=1)

    def pass_on():
        @pl.when(has_next)
        def _():
            out_copy.start()

    norm_row = norm_ref[...]
    update, counted = section(
        0, x1, joined(p_in), mem1, norm_row, counts_ref[ph + 1], out1, pass_on
    )
    mem2[...] = mem1[...] + update
    norm_row = norm_row + counted

    @pl.when(ph == 0)
    def _():
        for copy in pf_copies + fresh_copies:
            copy.wait_recv()
        loads[8].wait()
        p_second[...] = joined(p_fresh)

    @pl.when(has_prev)
    def _():
        pq_copy.wait_recv()
        out_copy.wait_recv()

    row_copies = []

    def hand_out():
        for d in range(1, n):
            copy = to_peer(
                ROWS, d, out2.at[block(peers[d])], rows_out.at[0, :, columns(me)]
            )
            copy.start()
            row_copies.append(copy)
        own_out.start()

    own_out = here(9, out2.at[block(me)], rows_out.at[0, :, columns(me)])
    update, counted = section(
        1, x2, p_second[...], mem2, norm_row, counts_ref[ph], out2, hand_out
    )
    memory_out[0] = mem2[...] + update
    norm_out[...] = norm_row + counted

    own_out.wait()
    for copy in row_copies:
        copy.wait()
    for copy in sent:
        copy.wait_send()

    @pl.when(ph == 0)
    def _():
        for copy in pf_copies + fresh_copies:
            copy.wait_send()

    @pl.when(has_prev)
    def _():
        weight_copy.wait_send()

    @pl.when(has_next)
    def _():
        out_copy.wait_send()
        pq_copy.wait_send()


def by_columns(n, n_phase, *args):
    phase_rows, memory, w_memq, w_kv, w_out = (args[0], args[3], args[5], args[8], args[9])
    rows, width = phase_rows.shape[1:]
    cols, depth, kv_cols = width // n, w_memq.shape[2], w_kv.shape[2]
    states, seg = memory.shape[1], n * rows
    half, full = jnp.bfloat16, jnp.float32
    select = jnp.asarray(selection(depth))
    any_space = pl.BlockSpec(memory_space=pl.ANY)
    vmem = pl.BlockSpec(memory_space=pltpu.VMEM)
    smem = pl.BlockSpec(memory_space=pltpu.SMEM)
    scratch = [
        ((seg, cols), half),
        ((seg, cols), half),
        ((rows, width), half),
        ((rows, width), half),
        ((width, depth), half),
        ((width, depth), half),
        ((cols, kv_cols), half),
        ((n, HEAD_DIM, cols), half),
        ((states, cols), full),
        ((states, cols), full),
        ((depth, width), half),
        ((depth, width), half),
        ((depth, cols), half),
        ((n, depth, rows), full),
        ((n, depth, rows), full),
        ((depth, seg), full),
        ((depth, seg), full),
        ((seg, cols), full),
        ((2, n, seg, 2 * HEAD_DIM), half),
        ((2, n, seg, 2 * HEAD_DIM), half),
        ((2, n, 8, seg), full),
        ((2, n, seg, HEAD_DIM), half),
        ((2, n, 2 * depth, seg), full),
        ((seg, cols), half),
        ((seg, cols), half),
    ]
    flops = 4 * seg * cols * (4 * states + kv_cols + n * HEAD_DIM)
    return pl.pallas_call(
        functools.partial(columns_kernel, n, n_phase),
        out_shape=(
            jax.ShapeDtypeStruct(phase_rows.shape, half),
            jax.ShapeDtypeStruct(memory.shape, full),
            jax.ShapeDtypeStruct(args[4].shape, full),
        ),
        in_specs=[any_space, any_space, smem, any_space, vmem]
        + [any_space, any_space, vmem, any_space, any_space, vmem],
        out_specs=(any_space, vmem, vmem),
        scratch_shapes=[pltpu.VMEM(shape, kind) for shape, kind in scratch]
        + [
            pltpu.SemaphoreType.DMA((N_KINDS, n)),
            pltpu.SemaphoreType.DMA((N_KINDS, n)),
            pltpu.SemaphoreType.DMA((3,)),
            pltpu.SemaphoreType.DMA((3,)),
            pltpu.SemaphoreType.DMA((10,)),
        ],
        cost_estimate=pl.CostEstimate(
            flops=flops, bytes_accessed=6_000_000, transcendentals=2 * seg * seg
        ),
        compiler_params=pltpu.CompilerParams(
            collective_id=0, has_side_effects=True, vmem_limit_bytes=48 * 1024 * 1024
        ),
    )(*args, select)


def dispatch(n, n_phase, *args):
    rows, width = args[0].shape[1:]
    heads = n * args[9].shape[1] // HEAD_DIM
    fits = heads == n and width % (n * 128) == 0 and rows % 16 == 0 and (n * rows) % 128 == 0
    if fits and n * rows <= 512:
        return by_columns(n, n_phase, *args)
    return per_device(*args)


def solution(mesh):
    return jax.shard_map(
        functools.partial(dispatch, mesh.shape["seq"], mesh.shape["phase"]),
        mesh=mesh,
        in_specs=(
            P("phase", ("groups", "seq"), None),
            P(("groups", "seq"), None),
            P("groups"),
            P("phase", "groups", "seq"),
            P("phase", "groups"),
            P("phase", None, None),
            P("phase", None, None),
            P("phase", None),
            P("phase", "seq", None),
            P("phase", "seq", None),
        ),
        out_specs=(
            P("phase", ("groups", "seq"), None),
            P("phase", "groups", "seq"),
            P("phase", "groups"),
        ),
        check_vma=False,
    )
```

```python
import functools
import math

import jax
import jax.numpy as jnp
from jax import lax
from jax.experimental import pallas as pl
from jax.experimental.pallas import tpu as pltpu
from jax.sharding import PartitionSpec as P

HEAD_DIM = 128


PRECISE = lax.Precision.HIGHEST


def from_behind(value, axis, steps):
    count = lax.axis_size(axis)
    first, last = (max(0, -steps), min(count, count - steps))
    return lax.ppermute(value, axis, [(source, source + steps) for source in range(first, last)])


def features(projected):
    halves = jnp.concatenate([jax.nn.relu(projected), jax.nn.relu(-projected)], axis=-1)
    return jnp.concatenate(
        [halves * jnp.roll(halves, offset, axis=-1) for offset in (1, 2, 3)], axis=-1
    )


def recall(feature_rows, memory_state, norm_state):
    numerator = jnp.dot(feature_rows, memory_state, precision=PRECISE)
    denominator = jnp.dot(feature_rows, norm_state, precision=PRECISE) + 1.0
    return numerator / denominator[:, None]


def attend(keyval, valid_count, position, head_count):
    token_rows = keyval.shape[0]
    kv_width = head_count * HEAD_DIM
    queries = keyval[:, :kv_width].reshape(token_rows, head_count, HEAD_DIM)
    divisor = math.sqrt(HEAD_DIM)

    def absorb_block(running, block_rows, first_row):
        highest, summed, weighted = running
        piece_rows = block_rows.shape[0]
        piece_keys = block_rows[:, :kv_width].reshape(piece_rows, head_count, HEAD_DIM)
        piece_values = (
            block_rows[:, kv_width:].reshape(piece_rows, head_count, HEAD_DIM).astype(jnp.float32)
        )
        scores = (
            jnp.einsum("qhd,khd->hqk", queries, piece_keys, preferred_element_type=jnp.float32)
            / divisor
        )
        key_position = first_row + jnp.arange(piece_rows)
        allowed = (key_position[None, :] < valid_count) & (
            key_position[None, :] != position[:, None]
        )
        masked = jnp.where(allowed[None], scores, -1e30)
        new_highest = jnp.maximum(highest, jnp.max(masked, axis=-1))
        weights = jnp.where(allowed[None], jnp.exp(masked - new_highest[..., None]), 0.0)
        shrink = jnp.exp(highest - new_highest)
        summed = summed * shrink + jnp.sum(weights, axis=-1)
        weighted = weighted * shrink[..., None] + jnp.einsum(
            "hqk,khd->hqd", weights, piece_values, precision=PRECISE
        )
        return (new_highest, summed, weighted)

    initial = (
        jnp.full((head_count, token_rows), -1e30, jnp.float32),
        jnp.zeros((head_count, token_rows), jnp.float32),
        jnp.zeros((head_count, token_rows, HEAD_DIM), jnp.float32),
    )
    running = initial
    shard_rows = lax.all_gather(keyval, "seq", axis=0, tiled=True)
    piece_rows = shard_rows.shape[0]
    block = piece_rows
    while block > 1024 and block % 2 == 0:
        block = block // 2
    block_count = piece_rows // block
    blocks = shard_rows.reshape(block_count, block, shard_rows.shape[1])
    starts = block * jnp.arange(block_count, dtype=jnp.int32)

    def one_block(carry, item):
        block_rows, block_start = item
        return (absorb_block(carry, block_rows, block_start), None)

    running, unused = lax.scan(one_block, running, (blocks, starts))
    highest, summed, weighted = running
    attended = weighted / summed[..., None]
    return jnp.transpose(attended, (1, 0, 2)).reshape(token_rows, kv_width).astype(jnp.bfloat16)


def run_section(in_rows, valid_count, reader, position, params):
    w_memq, w_memk, norm_gain, weights_full, out_full = params
    head_count = out_full.shape[0] // HEAD_DIM
    query_features = features(jnp.dot(in_rows, w_memq, preferred_element_type=jnp.float32))
    residual = in_rows.astype(jnp.float32) + reader(query_features)
    inverse_rms = lax.rsqrt(jnp.mean(residual * residual, axis=-1, keepdims=True) + 1e-05)
    normed = (residual * inverse_rms * norm_gain).astype(jnp.bfloat16)
    keyval = jnp.dot(normed, weights_full, preferred_element_type=jnp.float32).astype(jnp.bfloat16)
    attended = attend(keyval, valid_count, position, head_count)
    output = (residual + jnp.dot(attended, out_full, preferred_element_type=jnp.float32)).astype(
        jnp.bfloat16
    )
    key_features = features(jnp.dot(output, w_memk, preferred_element_type=jnp.float32))
    live_rows = (position < valid_count).astype(jnp.float32)[:, None]
    correction = (output.astype(jnp.float32) - reader(key_features)) * live_rows
    key_features = key_features * live_rows
    update = lax.dot_general(key_features, correction, (((0,), (0,)), ((), ())), precision=PRECISE)
    return (output, update, jnp.sum(key_features, axis=0))


def per_device(
    phase_rows, fresh_rows, token_counts, memory, normalizer, w_memq, w_memk, norm_gain, w_kv, w_out
):
    token_rows = phase_rows.shape[1]
    section_index = lax.axis_index("phase")
    seq_index = lax.axis_index("seq")
    position = seq_index * token_rows + jnp.arange(token_rows)
    weights_full, out_full = (
        lax.all_gather(w_kv[0], "seq", axis=0, tiled=True),
        lax.all_gather(w_out[0], "seq", axis=0, tiled=True),
    )
    memory_cols = memory[0]
    column_width = memory_cols.shape[1]
    memory_full = lax.all_gather(memory_cols, "seq", axis=1, tiled=True)
    norm_now = normalizer[0]
    params = (w_memq[0], w_memk[0], norm_gain[0], weights_full, out_full)

    def first_reader(feature_rows):
        return recall(feature_rows, memory_full, norm_now)

    first_rows, first_update, first_counts = run_section(
        phase_rows[0], token_counts[section_index + 1], first_reader, position, params
    )
    summed, counted = (
        lax.psum(first_update.astype(jnp.bfloat16), "seq").astype(jnp.float32),
        lax.psum(first_counts.astype(jnp.bfloat16), "seq").astype(jnp.float32),
    )
    later_full = memory_full + summed
    later_norm = norm_now + counted
    later_cols = lax.dynamic_slice_in_dim(later_full, seq_index * column_width, column_width, 1)

    def later_reader(feature_rows):
        return recall(feature_rows, later_full, later_norm)

    incoming = from_behind(first_rows, "phase", 1)
    second_in = jnp.where(section_index == 0, fresh_rows, incoming)
    second_rows, second_update, second_counts = run_section(
        second_in, token_counts[section_index], later_reader, position, params
    )
    final_share = lax.psum_scatter(
        second_update.astype(jnp.bfloat16), "seq", scatter_dimension=1, tiled=True
    ).astype(jnp.float32)
    final_counts = lax.psum(second_counts.astype(jnp.bfloat16), "seq").astype(jnp.float32)
    return (second_rows[None], (later_cols + final_share)[None], (later_norm + final_counts)[None])


MESH = pl.DeviceIdType.MESH
NN = (((1,), (0,)), ((), ()))
NT = (((1,), (1,)), ((), ()))
TN = (((0,), (0,)), ((), ()))
(X_IN, P_IN, WOUT, FRESH, P_FRESH, KV, SQ, ATT, PK) = range(9)
ROWS = 13
N_KINDS = 14


def mxu(left, right, dims, precision=None):
    return lax.dot_general(
        left, right, dims, precision=precision, preferred_element_type=jnp.float32
    )


def selection(key_dim):
    width = 2 * key_dim
    shape = (6 * width, key_dim)
    number = lax.broadcasted_iota(jnp.int32, shape, 0)
    source = lax.broadcasted_iota(jnp.int32, shape, 1)
    second = number >= 3 * width
    within = jnp.where(second, number - 3 * width, number)
    offset = 1 + (within >= width).astype(jnp.int32) + (within >= 2 * width).astype(jnp.int32)
    place = within - (offset - 1) * width
    turned = place - offset
    turned = jnp.where(turned < 0, turned + width, turned)
    entry = jnp.where(second, turned, place)
    return (entry == source).astype(jnp.float32) - (entry == source + key_dim).astype(jnp.float32)


def columns_kernel(
    n,
    n_phase,
    rows_hbm,
    fresh_hbm,
    counts_ref,
    memory_hbm,
    norm_ref,
    query_w,
    key_w,
    gain_ref,
    wkv_hbm,
    wout_hbm,
    rows_out,
    memory_out,
    norm_out,
    x1,
    x2,
    own_rows,
    own_fresh,
    wkv,
    wout,
    mem1,
    mem2,
    next_w,
    p_in,
    p_fresh,
    p_second,
    pq_out,
    resid,
    kv_out,
    kv_in,
    squares,
    att,
    pk,
    out1,
    out2,
    send,
    recv,
    phase_send,
    phase_recv,
    group_send,
    group_recv,
    local,
):
    me, ph = lax.axis_index("seq"), lax.axis_index("phase")
    rows, cols = own_rows.shape[0], x1.shape[1]
    width, depth = own_rows.shape[1], next_w.shape[0]
    kvw = wkv.shape[1] // 2
    seg = n * rows
    peers = [lax.rem(me + d, n) for d in range(n)]
    origins = [lax.rem(me - d + n, n) for d in range(n)]
    has_next, has_prev = ph < n_phase - 1, ph > 0

    def columns(index):
        return pl.ds(pl.multiple_of(index * cols, cols), cols)

    def block(index):
        return pl.ds(pl.multiple_of(index * rows, rows), rows)

    def head(index, first=0):
        return pl.ds(pl.multiple_of(first + index * HEAD_DIM, HEAD_DIM), HEAD_DIM)

    def to_peer(kind, d, src, dst):
        return pltpu.make_async_remote_copy(
            src_ref=src,
            dst_ref=dst,
            send_sem=send.at[kind, d],
            recv_sem=recv.at[kind, d],
            device_id={"seq": peers[d]},
            device_id_type=MESH,
        )

    def to_phase(kind, step, src, dst):
        return pltpu.make_async_remote_copy(
            src_ref=src,
            dst_ref=dst,
            send_sem=phase_send.at[kind],
            recv_sem=phase_recv.at[kind],
            device_id={"phase": ph + step},
            device_id_type=MESH,
        )

    def here(number, src, dst):
        return pltpu.make_async_copy(src, dst, local.at[number])

    own_load = here(0, rows_hbm.at[0], own_rows)
    memory_load = here(1, memory_hbm.at[0], mem1)
    x_load = here(2, rows_hbm.at[0, :, columns(me)], x1.at[block(me)])
    kv_load = here(3, wkv_hbm.at[0], wkv)
    wout_load = here(4, wout_hbm.at[0, :, columns(me)], wout.at[me])
    own_fresh_load = here(5, fresh_hbm, own_fresh)
    fresh_load = here(6, fresh_hbm.at[:, columns(me)], x2.at[block(me)])
    for copy in (own_load, x_load, own_fresh_load, memory_load, kv_load, wout_load):
        copy.start()

    barrier = pltpu.get_barrier_semaphore()
    for d in range(1, n):
        pl.semaphore_signal(barrier, inc=1, device_id={"seq": peers[d]}, device_id_type=MESH)

    @pl.when(has_next)
    def _():
        pl.semaphore_signal(barrier, inc=1, device_id={"phase": ph + 1}, device_id_type=MESH)

    @pl.when(has_prev)
    def _():
        pl.semaphore_signal(barrier, inc=1, device_id={"phase": ph - 1}, device_id_type=MESH)

    other = 1 - lax.axis_index("groups")
    pl.semaphore_signal(barrier, inc=1, device_id={"groups": other}, device_id_type=MESH)
    pl.semaphore_wait(barrier, n + has_next.astype(jnp.int32) + has_prev.astype(jnp.int32))

    sent = []
    half_rows = wout.shape[1] // 2
    half = pl.ds(pl.multiple_of((1 - other) * half_rows, half_rows), half_rows)
    x_copies = [
        to_peer(X_IN, d, rows_hbm.at[0, :, columns(peers[d])], x1.at[block(me)])
        for d in range(1, n)
    ]
    fresh_copies = [
        to_peer(FRESH, d, fresh_hbm.at[:, columns(peers[d])], x2.at[block(me)])
        for d in range(1, n)
    ]
    wout_copies = [
        to_peer(WOUT, d, wout_hbm.at[0, half, columns(peers[d])], wout.at[me, half])
        for d in range(1, n)
    ]
    across_copies = [
        pltpu.make_async_remote_copy(
            src_ref=wout.at[origins[d], half],
            dst_ref=wout.at[origins[d], half],
            send_sem=group_send.at[d],
            recv_sem=group_recv.at[d],
            device_id={"groups": other},
            device_id_type=MESH,
        )
        for d in range(1, n)
    ]
    p_copies = [to_peer(P_IN, d, p_in.at[me], p_in.at[me]) for d in range(1, n)]
    pf_copies = [to_peer(P_FRESH, d, p_fresh.at[me], p_fresh.at[me]) for d in range(1, n)]
    for copy in x_copies:
        copy.start()
    sent += x_copies + wout_copies + across_copies + p_copies

    own_load.wait()
    p_in[me] = mxu(query_w[0], own_rows[...], NT)
    for copy in p_copies:
        copy.start()
    weight_copy = to_phase(0, -1, query_w.at[0, :, columns(me)], next_w)

    @pl.when(has_prev)
    def _():
        weight_copy.start()

    own_fresh_load.wait()

    @pl.when(ph == 0)
    def _():
        fresh_load.start()
        p_fresh[me] = mxu(query_w[0], own_fresh[...], NT)
        for copy in pf_copies:
            copy.start()

    for copy in wout_copies:
        copy.start()

    select = selection(depth)

    def across(projected):
        pairs = mxu(select, projected, NN, PRECISE)
        pairs = jnp.maximum(pairs, 0.0)
        half = pairs.shape[0] // 2
        return pairs[:half] * pairs[half:]

    def recalled(turned, mem_ref, norm_row):
        upright = turned.T
        scale = jnp.sum(upright * norm_row, axis=1, keepdims=True) + 1.0
        found = mxu(upright.astype(jnp.bfloat16), mem_ref[...].astype(jnp.bfloat16), NN)
        return found / scale, upright

    def section(step, x_ref, projected, mem_ref, norm_row, valid, out_ref, after_output):
        base = 4 * step
        found, _ = recalled(across(projected), mem_ref, norm_row)
        residual = x_ref[...].astype(jnp.float32) + found
        resid[...] = residual
        square = jnp.sum(residual * residual, axis=1, keepdims=True)
        squares[step, me] = jnp.broadcast_to(square, (seg, 128)).T[:8]
        copies = []
        for d in range(1, n):
            copy = to_peer(SQ + base, d, squares.at[step, me], squares.at[step, me])
            copy.start()
            copies.append(copy)
        scaled = (residual * gain_ref[:, columns(me)]).astype(jnp.bfloat16)
        if step == 0:
            kv_load.wait()

        def part(index):
            keys = mxu(scaled, wkv[:, head(index)], NN)
            values = mxu(scaled, wkv[:, head(index, kvw)], NN)
            return jnp.concatenate([keys, values], axis=1)

        for d in range(1, n):
            kv_out[step, d] = part(peers[d]).astype(jnp.bfloat16)
            copy = to_peer(KV + base, d, kv_out.at[step, d], kv_in.at[step, me])
            copy.start()
            copies.append(copy)
        total = part(me)
        if step == 0:
            for copy, relay in zip(wout_copies, across_copies):
                copy.wait_recv()
                relay.start()
        sums = squares[step, me]
        for copy in copies:
            copy.wait_recv()
        for d in range(1, n):
            total = total + kv_in[step, origins[d]].astype(jnp.float32)
            sums = sums + squares[step, origins[d]]
        inverse = lax.rsqrt(sums[:1] / width + 1e-05)
        inverse = jnp.broadcast_to(inverse, (128, seg)).T
        keys = (total[:, :HEAD_DIM] * inverse).astype(jnp.bfloat16)
        values = (total[:, HEAD_DIM:] * inverse).astype(jnp.bfloat16)
        scores = mxu(keys, keys, NT) / math.sqrt(HEAD_DIM)
        row_at = lax.broadcasted_iota(jnp.int32, (seg, seg), 0)
        key_at = lax.broadcasted_iota(jnp.int32, (seg, seg), 1)
        scores = jnp.where((key_at < valid) & (key_at != row_at), scores, -1e30)
        weights = jnp.exp(scores - jnp.max(scores, axis=1, keepdims=True))
        weight_sum = jnp.sum(weights, axis=1, keepdims=True)
        attended = mxu(weights.astype(jnp.bfloat16), values, NN) / weight_sum
        att[step, me] = attended.astype(jnp.bfloat16)
        att_copies = []
        for d in range(1, n):
            copy = to_peer(ATT + base, d, att.at[step, me], att.at[step, me])
            copy.start()
            att_copies.append(copy)
        if step == 0:
            wout_load.wait()
            for copy in across_copies:
                copy.wait_recv()
        resid[...] += mxu(att[step, me], wout[me], NN)
        for d in range(1, n):
            att_copies[d - 1].wait_recv()
            resid[...] += mxu(att[step, origins[d]], wout[origins[d]], NN)
        output = resid[...].astype(jnp.bfloat16)
        out_ref[...] = output
        if step == 0:

            @pl.when(has_next)
            def _():
                weight_in.wait_recv()

            pk[step, me, pl.ds(depth, depth)] = mxu(next_w[...], output, NT)
        pk[step, me, pl.ds(0, depth)] = mxu(key_w[0, :, columns(me)], output, NT)
        taken = pl.ds(0, (2 - step) * depth)
        pk_copies = []
        for d in range(1, n):
            copy = to_peer(PK + base, d, pk.at[step, me, taken], pk.at[step, me, taken])
            copy.start()
            pk_copies.append(copy)
        after_output()
        for copy in pk_copies:
            copy.wait_recv()
        projected = pk[step, 0, taken]
        for index in range(1, n):
            projected = projected + pk[step, index, taken]
        if step == 0:
            pq_out[...] = projected[depth:]

            @pl.when(has_next)
            def _():
                pq_copy.start()

        turned = across(projected[:depth])
        found, upright = recalled(turned, mem_ref, norm_row)
        live = (lax.broadcasted_iota(jnp.int32, (seg, 1), 0) < valid).astype(jnp.float32)
        correction = (out_ref[...].astype(jnp.float32) - found) * live
        update = mxu(turned.astype(jnp.bfloat16), correction.astype(jnp.bfloat16), NN)
        counted = jnp.sum(upright * live, axis=0, keepdims=True)
        sent.extend(copies + att_copies + pk_copies)
        return update, counted

    weight_in = to_phase(0, -1, query_w.at[0, :, columns(me)], next_w)
    out_copy = to_phase(1, 1, out1, x2)
    pq_copy = to_phase(2, 1, pq_out, p_second)

    @pl.when(ph == n_phase - 1)
    def _():
        next_w[...] = jnp.zeros_like(next_w)

    memory_load.wait()
    x_load.wait()
    for copy in p_copies + x_copies:
        copy.wait_recv()

    def joined(ref):
        return jnp.concatenate([ref[index] for index in range(n)], axis=1)

    def pass_on():
        @pl.when(has_next)
        def _():
            out_copy.start()

        @pl.when(ph == 0)
        def _():
            for copy in fresh_copies:
                copy.start()

    norm_row = norm_ref[...]
    update, counted = section(
        0, x1, joined(p_in), mem1, norm_row, counts_ref[ph + 1], out1, pass_on
    )
    mem2[...] = mem1[...] + update
    norm_row = norm_row + counted

    @pl.when(ph == 0)
    def _():
        for copy in pf_copies + fresh_copies:
            copy.wait_recv()
        fresh_load.wait()
        p_second[...] = joined(p_fresh)

    @pl.when(has_prev)
    def _():
        pq_copy.wait_recv()
        out_copy.wait_recv()

    row_copies = []

    def hand_out():
        for d in range(1, n):
            copy = to_peer(
                ROWS, d, out2.at[block(peers[d])], rows_out.at[0, :, columns(me)]
            )
            copy.start()
            row_copies.append(copy)
        own_out.start()

    own_out = here(7, out2.at[block(me)], rows_out.at[0, :, columns(me)])
    update, counted = section(
        1, x2, p_second[...], mem2, norm_row, counts_ref[ph], out2, hand_out
    )
    memory_out[0] = mem2[...] + update
    norm_out[...] = norm_row + counted

    own_out.wait()
    for copy in row_copies:
        copy.wait()
    for copy in sent:
        copy.wait_send()

    @pl.when(ph == 0)
    def _():
        for copy in pf_copies + fresh_copies:
            copy.wait_send()

    @pl.when(has_prev)
    def _():
        weight_copy.wait_send()

    @pl.when(has_next)
    def _():
        out_copy.wait_send()
        pq_copy.wait_send()


def by_columns(n, n_phase, *args):
    phase_rows, memory, w_memq, w_kv, w_out = (args[0], args[3], args[5], args[8], args[9])
    rows, width = phase_rows.shape[1:]
    cols, depth, kv_cols = width // n, w_memq.shape[2], w_kv.shape[2]
    states, seg = memory.shape[1], n * rows
    half, full = jnp.bfloat16, jnp.float32
    w_memk = args[6]
    args = args[:5] + (jnp.swapaxes(w_memq, 1, 2), jnp.swapaxes(w_memk, 1, 2)) + args[7:]
    any_space = pl.BlockSpec(memory_space=pltpu.HBM)
    vmem = pl.BlockSpec(memory_space=pltpu.VMEM)
    smem = pl.BlockSpec(memory_space=pltpu.SMEM)
    scratch = [
        ((seg, cols), half),
        ((seg, cols), half),
        ((rows, width), half),
        ((rows, width), half),
        ((cols, kv_cols), half),
        ((n, HEAD_DIM, cols), half),
        ((states, cols), full),
        ((states, cols), full),
        ((depth, cols), half),
        ((n, depth, rows), full),
        ((n, depth, rows), full),
        ((depth, seg), full),
        ((depth, seg), full),
        ((seg, cols), full),
        ((2, n, seg, 2 * HEAD_DIM), half),
        ((2, n, seg, 2 * HEAD_DIM), half),
        ((2, n, 8, seg), full),
        ((2, n, seg, HEAD_DIM), half),
        ((2, n, 2 * depth, seg), full),
        ((seg, cols), half),
        ((seg, cols), half),
    ]
    flops = 4 * seg * cols * (4 * states + kv_cols + n * HEAD_DIM)
    return pl.pallas_call(
        functools.partial(columns_kernel, n, n_phase),
        out_shape=(
            jax.ShapeDtypeStruct(phase_rows.shape, half),
            jax.ShapeDtypeStruct(memory.shape, full),
            jax.ShapeDtypeStruct(args[4].shape, full),
        ),
        in_specs=[any_space, any_space, smem, any_space, vmem]
        + [vmem, vmem, vmem, any_space, any_space],
        out_specs=(any_space, vmem, vmem),
        scratch_shapes=[pltpu.VMEM(shape, kind) for shape, kind in scratch]
        + [
            pltpu.SemaphoreType.DMA((N_KINDS, n)),
            pltpu.SemaphoreType.DMA((N_KINDS, n)),
            pltpu.SemaphoreType.DMA((3,)),
            pltpu.SemaphoreType.DMA((3,)),
            pltpu.SemaphoreType.DMA((n,)),
            pltpu.SemaphoreType.DMA((n,)),
            pltpu.SemaphoreType.DMA((8,)),
        ],
        cost_estimate=pl.CostEstimate(
            flops=flops, bytes_accessed=6_000_000, transcendentals=2 * seg * seg
        ),
        compiler_params=pltpu.CompilerParams(
            collective_id=0, has_side_effects=True, vmem_limit_bytes=60 * 1024 * 1024
        ),
    )(*args)


def dispatch(n, n_phase, n_groups, *args):
    rows, width = args[0].shape[1:]
    heads = n * args[9].shape[1] // HEAD_DIM
    fits = heads == n and width % (n * 128) == 0 and rows % 16 == 0 and (n * rows) % 128 == 0
    if fits and n_groups == 2 and n * rows <= 512:
        return by_columns(n, n_phase, *args)
    return per_device(*args)


def solution(mesh):
    return jax.shard_map(
        functools.partial(dispatch, mesh.shape["seq"], mesh.shape["phase"], mesh.shape["groups"]),
        mesh=mesh,
        in_specs=(
            P("phase", ("groups", "seq"), None),
            P(("groups", "seq"), None),
            P("groups"),
            P("phase", "groups", "seq"),
            P("phase", "groups"),
            P("phase", None, None),
            P("phase", None, None),
            P("phase", None),
            P("phase", "seq", None),
            P("phase", "seq", None),
        ),
        out_specs=(
            P("phase", ("groups", "seq"), None),
            P("phase", "groups", "seq"),
            P("phase", "groups"),
        ),
        check_vma=False,
    )
```

```python
import functools
import math

import jax
import jax.numpy as jnp
from jax import lax
from jax.experimental import pallas as pl
from jax.experimental.pallas import tpu as pltpu
from jax.sharding import PartitionSpec as P

HEAD_DIM = 128


PRECISE = lax.Precision.HIGHEST


def from_behind(value, axis, steps):
    count = lax.axis_size(axis)
    first, last = (max(0, -steps), min(count, count - steps))
    return lax.ppermute(value, axis, [(source, source + steps) for source in range(first, last)])


def features(projected):
    halves = jnp.concatenate([jax.nn.relu(projected), jax.nn.relu(-projected)], axis=-1)
    return jnp.concatenate(
        [halves * jnp.roll(halves, offset, axis=-1) for offset in (1, 2, 3)], axis=-1
    )


def recall(feature_rows, memory_state, norm_state):
    numerator = jnp.dot(feature_rows, memory_state, precision=PRECISE)
    denominator = jnp.dot(feature_rows, norm_state, precision=PRECISE) + 1.0
    return numerator / denominator[:, None]


def attend(keyval, valid_count, position, head_count):
    token_rows = keyval.shape[0]
    kv_width = head_count * HEAD_DIM
    queries = keyval[:, :kv_width].reshape(token_rows, head_count, HEAD_DIM)
    divisor = math.sqrt(HEAD_DIM)

    def absorb_block(running, block_rows, first_row):
        highest, summed, weighted = running
        piece_rows = block_rows.shape[0]
        piece_keys = block_rows[:, :kv_width].reshape(piece_rows, head_count, HEAD_DIM)
        piece_values = (
            block_rows[:, kv_width:].reshape(piece_rows, head_count, HEAD_DIM).astype(jnp.float32)
        )
        scores = (
            jnp.einsum("qhd,khd->hqk", queries, piece_keys, preferred_element_type=jnp.float32)
            / divisor
        )
        key_position = first_row + jnp.arange(piece_rows)
        allowed = (key_position[None, :] < valid_count) & (
            key_position[None, :] != position[:, None]
        )
        masked = jnp.where(allowed[None], scores, -1e30)
        new_highest = jnp.maximum(highest, jnp.max(masked, axis=-1))
        weights = jnp.where(allowed[None], jnp.exp(masked - new_highest[..., None]), 0.0)
        shrink = jnp.exp(highest - new_highest)
        summed = summed * shrink + jnp.sum(weights, axis=-1)
        weighted = weighted * shrink[..., None] + jnp.einsum(
            "hqk,khd->hqd", weights, piece_values, precision=PRECISE
        )
        return (new_highest, summed, weighted)

    initial = (
        jnp.full((head_count, token_rows), -1e30, jnp.float32),
        jnp.zeros((head_count, token_rows), jnp.float32),
        jnp.zeros((head_count, token_rows, HEAD_DIM), jnp.float32),
    )
    running = initial
    shard_rows = lax.all_gather(keyval, "seq", axis=0, tiled=True)
    piece_rows = shard_rows.shape[0]
    block = piece_rows
    while block > 1024 and block % 2 == 0:
        block = block // 2
    block_count = piece_rows // block
    blocks = shard_rows.reshape(block_count, block, shard_rows.shape[1])
    starts = block * jnp.arange(block_count, dtype=jnp.int32)

    def one_block(carry, item):
        block_rows, block_start = item
        return (absorb_block(carry, block_rows, block_start), None)

    running, unused = lax.scan(one_block, running, (blocks, starts))
    highest, summed, weighted = running
    attended = weighted / summed[..., None]
    return jnp.transpose(attended, (1, 0, 2)).reshape(token_rows, kv_width).astype(jnp.bfloat16)


def run_section(in_rows, valid_count, reader, position, params):
    w_memq, w_memk, norm_gain, weights_full, out_full = params
    head_count = out_full.shape[0] // HEAD_DIM
    query_features = features(jnp.dot(in_rows, w_memq, preferred_element_type=jnp.float32))
    residual = in_rows.astype(jnp.float32) + reader(query_features)
    inverse_rms = lax.rsqrt(jnp.mean(residual * residual, axis=-1, keepdims=True) + 1e-05)
    normed = (residual * inverse_rms * norm_gain).astype(jnp.bfloat16)
    keyval = jnp.dot(normed, weights_full, preferred_element_type=jnp.float32).astype(jnp.bfloat16)
    attended = attend(keyval, valid_count, position, head_count)
    output = (residual + jnp.dot(attended, out_full, preferred_element_type=jnp.float32)).astype(
        jnp.bfloat16
    )
    key_features = features(jnp.dot(output, w_memk, preferred_element_type=jnp.float32))
    live_rows = (position < valid_count).astype(jnp.float32)[:, None]
    correction = (output.astype(jnp.float32) - reader(key_features)) * live_rows
    key_features = key_features * live_rows
    update = lax.dot_general(key_features, correction, (((0,), (0,)), ((), ())), precision=PRECISE)
    return (output, update, jnp.sum(key_features, axis=0))


def per_device(
    phase_rows, fresh_rows, token_counts, memory, normalizer, w_memq, w_memk, norm_gain, w_kv, w_out
):
    token_rows = phase_rows.shape[1]
    section_index = lax.axis_index("phase")
    seq_index = lax.axis_index("seq")
    position = seq_index * token_rows + jnp.arange(token_rows)
    weights_full, out_full = (
        lax.all_gather(w_kv[0], "seq", axis=0, tiled=True),
        lax.all_gather(w_out[0], "seq", axis=0, tiled=True),
    )
    memory_cols = memory[0]
    column_width = memory_cols.shape[1]
    memory_full = lax.all_gather(memory_cols, "seq", axis=1, tiled=True)
    norm_now = normalizer[0]
    params = (w_memq[0], w_memk[0], norm_gain[0], weights_full, out_full)

    def first_reader(feature_rows):
        return recall(feature_rows, memory_full, norm_now)

    first_rows, first_update, first_counts = run_section(
        phase_rows[0], token_counts[section_index + 1], first_reader, position, params
    )
    summed, counted = (
        lax.psum(first_update.astype(jnp.bfloat16), "seq").astype(jnp.float32),
        lax.psum(first_counts.astype(jnp.bfloat16), "seq").astype(jnp.float32),
    )
    later_full = memory_full + summed
    later_norm = norm_now + counted
    later_cols = lax.dynamic_slice_in_dim(later_full, seq_index * column_width, column_width, 1)

    def later_reader(feature_rows):
        return recall(feature_rows, later_full, later_norm)

    incoming = from_behind(first_rows, "phase", 1)
    second_in = jnp.where(section_index == 0, fresh_rows, incoming)
    second_rows, second_update, second_counts = run_section(
        second_in, token_counts[section_index], later_reader, position, params
    )
    final_share = lax.psum_scatter(
        second_update.astype(jnp.bfloat16), "seq", scatter_dimension=1, tiled=True
    ).astype(jnp.float32)
    final_counts = lax.psum(second_counts.astype(jnp.bfloat16), "seq").astype(jnp.float32)
    return (second_rows[None], (later_cols + final_share)[None], (later_norm + final_counts)[None])


MESH = pl.DeviceIdType.MESH
NN = (((1,), (0,)), ((), ()))
NT = (((1,), (1,)), ((), ()))
TN = (((0,), (0,)), ((), ()))
(X_IN, P_IN, WOUT, FRESH, P_FRESH, KV, SQ, ATT, PK) = range(9)
ROWS = 13
N_KINDS = 14


def mxu(left, right, dims, precision=None):
    return lax.dot_general(
        left, right, dims, precision=precision, preferred_element_type=jnp.float32
    )


def selection(key_dim):
    width = 2 * key_dim
    shape = (6 * width, key_dim)
    number = lax.broadcasted_iota(jnp.int32, shape, 0)
    source = lax.broadcasted_iota(jnp.int32, shape, 1)
    second = number >= 3 * width
    within = jnp.where(second, number - 3 * width, number)
    offset = 1 + (within >= width).astype(jnp.int32) + (within >= 2 * width).astype(jnp.int32)
    place = within - (offset - 1) * width
    turned = place - offset
    turned = jnp.where(turned < 0, turned + width, turned)
    entry = jnp.where(second, turned, place)
    return (entry == source).astype(jnp.float32) - (entry == source + key_dim).astype(jnp.float32)


def columns_kernel(
    n,
    n_phase,
    rows_hbm,
    fresh_hbm,
    counts_ref,
    memory_hbm,
    norm_ref,
    query_w,
    key_w,
    gain_ref,
    wkv_hbm,
    wout_hbm,
    rows_out,
    memory_out,
    norm_out,
    x1,
    x2,
    own_rows,
    own_fresh,
    wkv,
    wout,
    mem1,
    mem2,
    next_w,
    p_in,
    p_fresh,
    p_second,
    pq_out,
    resid,
    kv_out,
    kv_in,
    squares,
    att,
    pk,
    out1,
    out2,
    send,
    recv,
    phase_send,
    phase_recv,
    group_send,
    group_recv,
    local,
):
    me, ph = lax.axis_index("seq"), lax.axis_index("phase")
    rows, cols = own_rows.shape[0], x1.shape[1]
    width, depth = own_rows.shape[1], next_w.shape[0]
    kvw = wkv.shape[1] // 2
    seg = n * rows
    peers = [lax.rem(me + d, n) for d in range(n)]
    origins = [lax.rem(me - d + n, n) for d in range(n)]
    has_next, has_prev = ph < n_phase - 1, ph > 0

    def columns(index):
        return pl.ds(pl.multiple_of(index * cols, cols), cols)

    def block(index):
        return pl.ds(pl.multiple_of(index * rows, rows), rows)

    def head(index, first=0):
        return pl.ds(pl.multiple_of(first + index * HEAD_DIM, HEAD_DIM), HEAD_DIM)

    def to_peer(kind, d, src, dst):
        return pltpu.make_async_remote_copy(
            src_ref=src,
            dst_ref=dst,
            send_sem=send.at[kind, d],
            recv_sem=recv.at[kind, d],
            device_id={"seq": peers[d]},
            device_id_type=MESH,
        )

    def to_phase(kind, step, src, dst):
        return pltpu.make_async_remote_copy(
            src_ref=src,
            dst_ref=dst,
            send_sem=phase_send.at[kind],
            recv_sem=phase_recv.at[kind],
            device_id={"phase": ph + step},
            device_id_type=MESH,
        )

    def here(number, src, dst):
        return pltpu.make_async_copy(src, dst, local.at[number])

    own_load = here(0, rows_hbm.at[0], own_rows)
    memory_load = here(1, memory_hbm.at[0], mem1)
    x_load = here(2, rows_hbm.at[0, :, columns(me)], x1.at[block(me)])
    kv_load = here(3, wkv_hbm.at[0], wkv)
    wout_load = here(4, wout_hbm.at[0, :, columns(me)], wout.at[me])
    own_fresh_load = here(5, fresh_hbm, own_fresh)
    fresh_load = here(6, fresh_hbm.at[:, columns(me)], x2.at[block(me)])
    for copy in (own_load, x_load, own_fresh_load, memory_load, kv_load, wout_load):
        copy.start()

    barrier = pltpu.get_barrier_semaphore()
    for d in range(1, n):
        pl.semaphore_signal(barrier, inc=1, device_id={"seq": peers[d]}, device_id_type=MESH)

    @pl.when(has_next)
    def _():
        pl.semaphore_signal(barrier, inc=1, device_id={"phase": ph + 1}, device_id_type=MESH)

    @pl.when(has_prev)
    def _():
        pl.semaphore_signal(barrier, inc=1, device_id={"phase": ph - 1}, device_id_type=MESH)

    other = 1 - lax.axis_index("groups")
    pl.semaphore_signal(barrier, inc=1, device_id={"groups": other}, device_id_type=MESH)
    pl.semaphore_wait(barrier, n + has_next.astype(jnp.int32) + has_prev.astype(jnp.int32))

    sent = []
    half_rows = wout.shape[1] // 2
    half = pl.ds(pl.multiple_of((1 - other) * half_rows, half_rows), half_rows)
    x_copies = [
        to_peer(X_IN, d, rows_hbm.at[0, :, columns(peers[d])], x1.at[block(me)])
        for d in range(1, n)
    ]
    fresh_copies = [
        to_peer(FRESH, d, fresh_hbm.at[:, columns(peers[d])], x2.at[block(me)])
        for d in range(1, n)
    ]
    wout_copies = [
        to_peer(WOUT, d, wout_hbm.at[0, half, columns(peers[d])], wout.at[me, half])
        for d in range(1, n)
    ]
    across_copies = [
        pltpu.make_async_remote_copy(
            src_ref=wout.at[origins[d], half],
            dst_ref=wout.at[origins[d], half],
            send_sem=group_send.at[d],
            recv_sem=group_recv.at[d],
            device_id={"groups": other},
            device_id_type=MESH,
        )
        for d in range(1, n)
    ]
    p_copies = [to_peer(P_IN, d, p_in.at[me], p_in.at[me]) for d in range(1, n)]
    pf_copies = [to_peer(P_FRESH, d, p_fresh.at[me], p_fresh.at[me]) for d in range(1, n)]
    for copy in x_copies:
        copy.start()
    sent += x_copies + wout_copies + across_copies + p_copies

    own_load.wait()
    p_in[me] = mxu(query_w[0], own_rows[...], NT)
    for copy in p_copies:
        copy.start()
    weight_copy = to_phase(0, -1, query_w.at[0, :, columns(me)], next_w)

    @pl.when(has_prev)
    def _():
        weight_copy.start()

    own_fresh_load.wait()

    @pl.when(ph == 0)
    def _():
        fresh_load.start()
        p_fresh[me] = mxu(query_w[0], own_fresh[...], NT)
        for copy in pf_copies:
            copy.start()

    for copy in wout_copies:
        copy.start()

    select = selection(depth)

    def across(projected):
        pairs = mxu(select, projected, NN, PRECISE)
        pairs = jnp.maximum(pairs, 0.0)
        half = pairs.shape[0] // 2
        return pairs[:half] * pairs[half:]

    def recalled(turned, mem_ref, norm_row):
        upright = turned.T
        scale = jnp.sum(upright * norm_row, axis=1, keepdims=True) + 1.0
        found = mxu(upright.astype(jnp.bfloat16), mem_ref[...].astype(jnp.bfloat16), NN)
        return found / scale, upright

    def section(step, x_ref, projected, mem_ref, norm_row, valid, out_ref, after_output):
        base = 4 * step
        found, _ = recalled(across(projected), mem_ref, norm_row)
        residual = x_ref[...].astype(jnp.float32) + found
        resid[...] = residual
        square = jnp.sum(residual * residual, axis=1, keepdims=True)
        squares[step, me] = jnp.broadcast_to(square, (seg, 128)).T[:8]
        copies = []
        for d in range(1, n):
            copy = to_peer(SQ + base, d, squares.at[step, me], squares.at[step, me])
            copy.start()
            copies.append(copy)
        scaled = (residual * gain_ref[:, columns(me)]).astype(jnp.bfloat16)
        if step == 0:
            kv_load.wait()

        def part(index):
            keys = mxu(scaled, wkv[:, head(index)], NN)
            values = mxu(scaled, wkv[:, head(index, kvw)], NN)
            return jnp.concatenate([keys, values], axis=1)

        for d in range(1, n):
            kv_out[step, d] = part(peers[d]).astype(jnp.bfloat16)
            copy = to_peer(KV + base, d, kv_out.at[step, d], kv_in.at[step, me])
            copy.start()
            copies.append(copy)
        total = part(me)
        if step == 0:
            for copy, relay in zip(wout_copies, across_copies):
                copy.wait_recv()
                relay.start()
        sums = squares[step, me]
        for copy in copies:
            copy.wait_recv()
        for d in range(1, n):
            total = total + kv_in[step, origins[d]].astype(jnp.float32)
            sums = sums + squares[step, origins[d]]
        inverse = lax.rsqrt(sums[:1] / width + 1e-05)
        inverse = jnp.broadcast_to(inverse, (128, seg)).T
        keys = (total[:, :HEAD_DIM] * inverse).astype(jnp.bfloat16)
        values = (total[:, HEAD_DIM:] * inverse).astype(jnp.bfloat16)
        scores = mxu(keys, keys, NT) / math.sqrt(HEAD_DIM)
        row_at = lax.broadcasted_iota(jnp.int32, (seg, seg), 0)
        key_at = lax.broadcasted_iota(jnp.int32, (seg, seg), 1)
        scores = jnp.where((key_at < valid) & (key_at != row_at), scores, -1e30)
        weights = jnp.exp(scores - jnp.max(scores, axis=1, keepdims=True))
        weight_sum = jnp.sum(weights, axis=1, keepdims=True)
        attended = mxu(weights.astype(jnp.bfloat16), values, NN) / weight_sum
        att[step, me] = attended.astype(jnp.bfloat16)
        att_copies = []
        for d in range(1, n):
            copy = to_peer(ATT + base, d, att.at[step, me], att.at[step, me])
            copy.start()
            att_copies.append(copy)
        if step == 0:
            wout_load.wait()
            for copy in across_copies:
                copy.wait_recv()
        resid[...] += mxu(att[step, me], wout[me], NN)
        for d in range(1, n):
            att_copies[d - 1].wait_recv()
            resid[...] += mxu(att[step, origins[d]], wout[origins[d]], NN)
        output = resid[...].astype(jnp.bfloat16)
        out_ref[...] = output
        if step == 0:

            @pl.when(has_next)
            def _():
                weight_in.wait_recv()

            pk[step, me, pl.ds(depth, depth)] = mxu(next_w[...], output, NT).astype(jnp.bfloat16)
        pk[step, me, pl.ds(0, depth)] = mxu(key_w[0, :, columns(me)], output, NT).astype(jnp.bfloat16)
        taken = pl.ds(0, (2 - step) * depth)
        pk_copies = []
        for d in range(1, n):
            copy = to_peer(PK + base, d, pk.at[step, me, taken], pk.at[step, me, taken])
            copy.start()
            pk_copies.append(copy)
        after_output()
        for copy in pk_copies:
            copy.wait_recv()
        projected = pk[step, 0, taken].astype(jnp.float32)
        for index in range(1, n):
            projected = projected + pk[step, index, taken].astype(jnp.float32)
        if step == 0:
            pq_out[...] = projected[depth:]

            @pl.when(has_next)
            def _():
                pq_copy.start()

        turned = across(projected[:depth])
        found, upright = recalled(turned, mem_ref, norm_row)
        live = (lax.broadcasted_iota(jnp.int32, (seg, 1), 0) < valid).astype(jnp.float32)
        correction = (out_ref[...].astype(jnp.float32) - found) * live
        update = mxu(turned.astype(jnp.bfloat16), correction.astype(jnp.bfloat16), NN)
        counted = jnp.sum(upright * live, axis=0, keepdims=True)
        sent.extend(copies + att_copies + pk_copies)
        return update, counted

    weight_in = to_phase(0, -1, query_w.at[0, :, columns(me)], next_w)
    out_copy = to_phase(1, 1, out1, x2)
    pq_copy = to_phase(2, 1, pq_out, p_second)

    @pl.when(ph == n_phase - 1)
    def _():
        next_w[...] = jnp.zeros_like(next_w)

    memory_load.wait()
    x_load.wait()
    for copy in p_copies + x_copies:
        copy.wait_recv()

    def joined(ref):
        return jnp.concatenate([ref[index] for index in range(n)], axis=1)

    def pass_on():
        @pl.when(has_next)
        def _():
            out_copy.start()

        @pl.when(ph == 0)
        def _():
            for copy in fresh_copies:
                copy.start()

    norm_row = norm_ref[...]
    update, counted = section(
        0, x1, joined(p_in), mem1, norm_row, counts_ref[ph + 1], out1, pass_on
    )
    mem2[...] = mem1[...] + update
    norm_row = norm_row + counted

    @pl.when(ph == 0)
    def _():
        for copy in pf_copies + fresh_copies:
            copy.wait_recv()
        fresh_load.wait()
        p_second[...] = joined(p_fresh)

    @pl.when(has_prev)
    def _():
        pq_copy.wait_recv()
        out_copy.wait_recv()

    row_copies = []

    def hand_out():
        for d in range(1, n):
            copy = to_peer(
                ROWS, d, out2.at[block(peers[d])], rows_out.at[0, :, columns(me)]
            )
            copy.start()
            row_copies.append(copy)
        own_out.start()

    own_out = here(7, out2.at[block(me)], rows_out.at[0, :, columns(me)])
    update, counted = section(
        1, x2, p_second[...], mem2, norm_row, counts_ref[ph], out2, hand_out
    )
    memory_out[0] = mem2[...] + update
    norm_out[...] = norm_row + counted

    own_out.wait()
    for copy in row_copies:
        copy.wait()
    for copy in sent:
        copy.wait_send()

    @pl.when(ph == 0)
    def _():
        for copy in pf_copies + fresh_copies:
            copy.wait_send()

    @pl.when(has_prev)
    def _():
        weight_copy.wait_send()

    @pl.when(has_next)
    def _():
        out_copy.wait_send()
        pq_copy.wait_send()


def by_columns(n, n_phase, *args):
    phase_rows, memory, w_memq, w_kv, w_out = (args[0], args[3], args[5], args[8], args[9])
    rows, width = phase_rows.shape[1:]
    cols, depth, kv_cols = width // n, w_memq.shape[2], w_kv.shape[2]
    states, seg = memory.shape[1], n * rows
    half, full = jnp.bfloat16, jnp.float32
    w_memk = args[6]
    args = args[:5] + (jnp.swapaxes(w_memq, 1, 2), jnp.swapaxes(w_memk, 1, 2)) + args[7:]
    any_space = pl.BlockSpec(memory_space=pltpu.HBM)
    vmem = pl.BlockSpec(memory_space=pltpu.VMEM)
    smem = pl.BlockSpec(memory_space=pltpu.SMEM)
    scratch = [
        ((seg, cols), half),
        ((seg, cols), half),
        ((rows, width), half),
        ((rows, width), half),
        ((cols, kv_cols), half),
        ((n, HEAD_DIM, cols), half),
        ((states, cols), full),
        ((states, cols), full),
        ((depth, cols), half),
        ((n, depth, rows), full),
        ((n, depth, rows), full),
        ((depth, seg), full),
        ((depth, seg), full),
        ((seg, cols), full),
        ((2, n, seg, 2 * HEAD_DIM), half),
        ((2, n, seg, 2 * HEAD_DIM), half),
        ((2, n, 8, seg), full),
        ((2, n, seg, HEAD_DIM), half),
        ((2, n, 2 * depth, seg), half),
        ((seg, cols), half),
        ((seg, cols), half),
    ]
    flops = 4 * seg * cols * (4 * states + kv_cols + n * HEAD_DIM)
    return pl.pallas_call(
        functools.partial(columns_kernel, n, n_phase),
        out_shape=(
            jax.ShapeDtypeStruct(phase_rows.shape, half),
            jax.ShapeDtypeStruct(memory.shape, full),
            jax.ShapeDtypeStruct(args[4].shape, full),
        ),
        in_specs=[any_space, any_space, smem, any_space, vmem]
        + [vmem, vmem, vmem, any_space, any_space],
        out_specs=(any_space, vmem, vmem),
        scratch_shapes=[pltpu.VMEM(shape, kind) for shape, kind in scratch]
        + [
            pltpu.SemaphoreType.DMA((N_KINDS, n)),
            pltpu.SemaphoreType.DMA((N_KINDS, n)),
            pltpu.SemaphoreType.DMA((3,)),
            pltpu.SemaphoreType.DMA((3,)),
            pltpu.SemaphoreType.DMA((n,)),
            pltpu.SemaphoreType.DMA((n,)),
            pltpu.SemaphoreType.DMA((8,)),
        ],
        cost_estimate=pl.CostEstimate(
            flops=flops, bytes_accessed=6_000_000, transcendentals=2 * seg * seg
        ),
        compiler_params=pltpu.CompilerParams(
            collective_id=0, has_side_effects=True, vmem_limit_bytes=60 * 1024 * 1024
        ),
    )(*args)


def dispatch(n, n_phase, n_groups, *args):
    rows, width = args[0].shape[1:]
    heads = n * args[9].shape[1] // HEAD_DIM
    fits = heads == n and width % (n * 128) == 0 and rows % 16 == 0 and (n * rows) % 128 == 0
    if fits and n_groups == 2 and n * rows <= 512:
        return by_columns(n, n_phase, *args)
    return per_device(*args)


def solution(mesh):
    return jax.shard_map(
        functools.partial(dispatch, mesh.shape["seq"], mesh.shape["phase"], mesh.shape["groups"]),
        mesh=mesh,
        in_specs=(
            P("phase", ("groups", "seq"), None),
            P(("groups", "seq"), None),
            P("groups"),
            P("phase", "groups", "seq"),
            P("phase", "groups"),
            P("phase", None, None),
            P("phase", None, None),
            P("phase", None),
            P("phase", "seq", None),
            P("phase", "seq", None),
        ),
        out_specs=(
            P("phase", ("groups", "seq"), None),
            P("phase", "groups", "seq"),
            P("phase", "groups"),
        ),
        check_vma=False,
    )
```
